256 devices in a mesh: dp: 16 (over y_hi, z), expert: 16 (over y_lo, x, core).
Axes of the slice: x: 4, y: 4 (y_hi: 2, y_lo: 2; y = y_hi * 2 + y_lo), z: 8, core: 2. Of those that a mesh axis runs over, the one named last changes fastest.
Arguments:
- tokens: bfloat16 [2048, 196, 1024], P(('dp', 'expert')), may hold values from -4 to 4
- norm_gain: float32 [1024], replicated, may hold values from 0.1 to 1.9
- slot_weight: bfloat16 [1024, 16], replicated, may hold values from -2.0507812 to 2.0507812
- w_in: bfloat16 [16, 1024, 2048], P('expert', None, 'dp'), may hold values from -0.1875 to 0.1875
- w_out: bfloat16 [16, 2048, 1024], P('expert', 'dp'), may hold values from -0.125 to 0.125
- cotangent: bfloat16 [2048, 196, 1024], P(('dp', 'expert')), may hold values from -6 to 6
Outputs:
- d_tokens: bfloat16 [2048, 196, 1024], P(('dp', 'expert'))
- d_slot_weight: float32 [1024, 16], replicated
- d_gain: float32 [1024], replicated
- d_w_in: float32 [16, 1024, 2048], P('expert', None, 'dp')
- d_w_out: float32 [16, 2048, 1024], P('expert', 'dp')
The draws below stay inside these ranges and needn't reach their ends.
All inputs are finite; a program needn't handle non-finite values.
Results may differ from the reference program's by a relative error of at most 0.019.
The reference program's roundings to bfloat16 on the way (of `normed`, `slots`, `cot_slots`, `hidden`, `out_slots`, `d_act`, `grad_slots` and `d_logits`) count: a program that leaves them out, or rounds other values in their place, can miss the bound.
Values may be sent and summed in bfloat16 or wider, within the bound.
No kernel may reach another device: no remote copies, remote signals or barrier semaphores. Data moves between devices by JAX's collectives and lax.ppermute only.
A program may use at most 128 MiB of HBM per device.

```python
import jax
import jax.numpy as jnp
from jax import lax

D = 1024
FF = 2048
TOK = 196
EXPERTS = 16
IMAGES = 2048


def draw_tokens(key, part):
    key = jax.random.fold_in(key, 1)
    values = jnp.clip(jax.random.normal(key, (IMAGES, TOK, D), jnp.float32), -4.0, 4.0)
    return values.astype(jnp.bfloat16)


def draw_slot_weight(key, part):
    key = jax.random.fold_in(key, 3)
    values = jnp.clip(jax.random.normal(key, (D, EXPERTS), jnp.float32), -4.0, 4.0) * D ** (-0.5)
    return values.astype(jnp.bfloat16)


def shard_levels(rng, shape, cuts, smallest, largest):
    gain = 1.0
    for axis_at, blocks in cuts:
        heights = jax.random.uniform(jax.random.fold_in(jax.random.fold_in(rng, 6), axis_at), (blocks,), jnp.float32, smallest / len(cuts), largest / len(cuts))
        gain = gain * jnp.repeat(jnp.exp(heights), shape[axis_at] // blocks).reshape((-1,) + (1,) * (len(shape) - 1 - axis_at))
    return gain


def gaussian(rng, shape, width, most, split=(), kind=jnp.bfloat16):
    values = width * jax.random.normal(rng, shape, jnp.float32)
    if split:
        values = values * shard_levels(rng, shape, split, -0.22, 0.18)
    return jnp.clip(values, -most, most).astype(kind)


def setup_inputs(seed: int = 0) -> dict:
    key_list = jax.random.split(jax.random.key(seed), 7)
    return {
        "tokens": draw_tokens(jax.random.fold_in(key_list[6], 71), 0),
        "norm_gain": jnp.clip(1.0 + 0.18 * jax.random.normal(key_list[1], (D,), jnp.float32), 0.1, 1.9),
        "slot_weight": draw_slot_weight(jax.random.fold_in(key_list[6], 71), 0),
        "w_in": gaussian(key_list[3], (EXPERTS, D, FF), D ** -0.5, 0.1875, ((0, 16), (2, 16))),
        "w_out": gaussian(key_list[4], (EXPERTS, FF, D), FF ** -0.5, 0.125, ((0, 16), (1, 16))),
        "cotangent": gaussian(key_list[5], (IMAGES, TOK, D), 1.0, 6.0, ((0, 256),)),
    }


eps = 1e-06

def normalize(tokens, norm_gain):
    as_float = tokens.astype(jnp.float32)
    token_mean = lax.optimization_barrier(jnp.mean(as_float, axis=-1, keepdims=True))
    centred = as_float - token_mean
    inv_std = lax.rsqrt(lax.optimization_barrier(jnp.mean(centred * centred, axis=-1, keepdims=True)) + eps)
    x_hat = centred * inv_std
    normed = (x_hat * norm_gain).astype(jnp.bfloat16)
    return (normed, x_hat, inv_std)

def routing(normed, slot_weight):
    logits = jnp.einsum('btd,ds->bts', normed.astype(jnp.float32), slot_weight.astype(jnp.float32))
    return (jax.nn.softmax(logits, axis=1), jax.nn.softmax(logits, axis=2))

def front_pass(tokens, norm_gain, slot_weight, cotangent):
    normed, x_hat, inv_std = normalize(tokens, norm_gain)
    p_dispatch, p_combine = routing(normed, slot_weight)
    dispatch = p_dispatch.astype(jnp.bfloat16)
    combine = p_combine.astype(jnp.bfloat16)
    slots = jnp.einsum('bts,btd->sbd', dispatch.astype(jnp.float32), normed.astype(jnp.float32)).astype(jnp.bfloat16)
    cot_slots = jnp.einsum('bts,btd->sbd', combine.astype(jnp.float32), cotangent.astype(jnp.float32)).astype(jnp.bfloat16)
    return (slots, cot_slots)

def expert_math(slot_rows, cot_rows, first_layer, second_layer):
    pre_act = jnp.dot(slot_rows, first_layer, preferred_element_type=jnp.float32)
    hidden_f, gelu_back = jax.vjp(jax.nn.gelu, pre_act)
    hidden = hidden_f.astype(jnp.bfloat16)
    y_rows = jnp.dot(hidden, second_layer, preferred_element_type=jnp.float32).astype(jnp.bfloat16)
    d_hidden = jnp.dot(cot_rows, second_layer.T, preferred_element_type=jnp.float32)
    d_act = gelu_back(d_hidden)[0].astype(jnp.bfloat16)
    d_second = jnp.dot(hidden.T, cot_rows, preferred_element_type=jnp.float32)
    d_first = jnp.dot(slot_rows.T, d_act, preferred_element_type=jnp.float32)
    slot_grad = jnp.dot(d_act, first_layer.T, preferred_element_type=jnp.float32).astype(jnp.bfloat16)
    return (y_rows, slot_grad, d_first, d_second)

def back_pass(tokens, norm_gain, slot_weight, cotangent, out_slots, grad_slots):
    normed, x_hat, inv_std = normalize(tokens, norm_gain)
    p_dispatch, p_combine = routing(normed, slot_weight)
    dispatch = p_dispatch.astype(jnp.bfloat16)
    d_combine = jnp.einsum('btd,sbd->bts', cotangent.astype(jnp.float32), out_slots.astype(jnp.float32))
    d_dispatch = jnp.einsum('sbd,btd->bts', grad_slots.astype(jnp.float32), normed.astype(jnp.float32))
    from_combine = p_combine * (d_combine - lax.optimization_barrier(jnp.sum(p_combine * d_combine, axis=2, keepdims=True)))
    from_dispatch = p_dispatch * (d_dispatch - lax.optimization_barrier(jnp.sum(p_dispatch * d_dispatch, axis=1, keepdims=True)))
    d_logits = (from_combine + from_dispatch).astype(jnp.bfloat16)
    d_normed = jnp.einsum('bts,sbd->btd', dispatch.astype(jnp.float32), grad_slots.astype(jnp.float32))
    d_normed = d_normed + jnp.einsum('bts,ds->btd', d_logits.astype(jnp.float32), slot_weight.astype(jnp.float32))
    d_slot_weight = jnp.einsum('btd,bts->ds', normed.astype(jnp.float32), d_logits.astype(jnp.float32))
    d_gain = lax.optimization_barrier(jnp.sum(d_normed * x_hat, axis=(0, 1)))
    scaled = d_normed * norm_gain
    d_tokens = inv_std * (scaled - lax.optimization_barrier(jnp.mean(scaled, axis=-1, keepdims=True)) - x_hat * lax.optimization_barrier(jnp.mean(scaled * x_hat, axis=-1, keepdims=True)))
    return (d_tokens.astype(jnp.bfloat16), d_slot_weight, d_gain)

def reference(tokens, norm_gain, slot_weight, w_in, w_out, cotangent):

    def front_image(packed):
        image_tokens, image_cot = packed
        slots, cot_slots = front_pass(image_tokens[None], norm_gain, slot_weight, image_cot[None])
        return (slots[:, 0], cot_slots[:, 0])
    slots, cot_slots = lax.map(front_image, (tokens, cotangent))
    slots = jnp.swapaxes(slots, 0, 1)
    cot_slots = jnp.swapaxes(cot_slots, 0, 1)

    def expert_one(packed):
        return expert_math(packed[0], packed[1], packed[2], packed[3])
    out_slots, grad_slots, d_w_in, d_w_out = lax.map(expert_one, (slots, cot_slots, w_in, w_out))
    out_slots = jnp.swapaxes(out_slots, 0, 1)
    grad_slots = jnp.swapaxes(grad_slots, 0, 1)

    def back_image(carry, packed):
        image_tokens, image_cot, image_out, image_grad = packed
        d_image, d_weight, d_norm_gain = back_pass(image_tokens[None], norm_gain, slot_weight, image_cot[None], image_out[:, None], image_grad[:, None])
        return ((carry[0] + d_weight, carry[1] + d_norm_gain), d_image[0])
    start_carry = (jnp.zeros(slot_weight.shape, jnp.float32), jnp.zeros(norm_gain.shape, jnp.float32))
    totals, d_tokens = lax.scan(back_image, start_carry, (tokens, cotangent, out_slots, grad_slots))
    return (d_tokens, totals[0], totals[1], d_w_in, d_w_out)
```

```python
import jax
import jax.numpy as jnp
from jax import lax
from jax.experimental import pallas as pl
from jax.experimental.pallas import tpu as pltpu
from jax.sharding import Mesh
from jax.sharding import PartitionSpec as P

eps = 1e-06
f32 = jnp.float32
bf16 = jnp.bfloat16
VMEM = 40 * 1024 * 1024


def dot(a, b, ca, cb):
    return lax.dot_general(a, b, (((ca,), (cb,)), ((), ())), preferred_element_type=f32)


def front_kernel(
    x_ref, c_ref, gain_ref, wrep_ref, out_ref, normed_ref, pd_ref, pc_ref, lg_ref, st_ref, acc_s, acc_c
):
    b = pl.program_id(0)
    images = pl.num_programs(0)
    slots, rows, features = out_ref.shape[1:]
    x = x_ref[0].astype(f32)
    mu = jnp.mean(x, axis=-1, keepdims=True)
    xc = x - mu
    inv = lax.rsqrt(jnp.mean(xc * xc, axis=-1, keepdims=True) + eps)
    normed = (xc * inv * gain_ref[...]).astype(bf16)
    normed_ref[0] = normed
    logits = dot(normed, wrep_ref[...], 1, 0)
    lane = lax.broadcasted_iota(jnp.int32, logits.shape, 1)
    mine = lax.rem(lane, rows // 2) == b
    ed = jnp.exp(logits - jnp.max(logits, axis=0, keepdims=True))
    pd = jnp.where(mine, ed / jnp.sum(ed, axis=0, keepdims=True), 0.0)
    ec = jnp.where(mine, jnp.exp(logits - jnp.max(logits, axis=1, keepdims=True)), 0.0)
    pc = ec / jnp.sum(ec, axis=1, keepdims=True)
    pd_ref[0] = pd
    pc_ref[0] = pc
    lg_ref[0] = logits
    st_ref[0] = jnp.where(lane == 0, mu, inv)

    @pl.when(b == 0)
    def _():
        acc_s[...] = jnp.zeros_like(acc_s)
        acc_c[...] = jnp.zeros_like(acc_c)

    acc_s[...] += dot(pd.astype(bf16), normed, 0, 0)
    acc_c[...] += dot(pc.astype(bf16), c_ref[0], 0, 0)

    @pl.when(b == images - 1)
    def _():
        both = jnp.concatenate(
            [
                acc_s[...].reshape(slots, rows // 2, features),
                acc_c[...].reshape(slots, rows // 2, features),
            ],
            axis=1,
        ).astype(bf16)
        for copy in range(out_ref.shape[0]):
            out_ref[copy] = both


def front(tokens, norm_gain, wrep, cotangent, copies):
    images, tok, features = tokens.shape
    wide = wrep.shape[1]
    slots = wide // images
    image = pl.BlockSpec((1, tok, features), lambda b: (b, 0, 0))
    narrow = pl.BlockSpec((1, tok, wide), lambda b: (b, 0, 0))
    routing = jax.ShapeDtypeStruct((images, tok, wide), f32)
    return pl.pallas_call(
        front_kernel,
        grid=(images,),
        in_specs=[
            image,
            image,
            pl.BlockSpec((1, features), lambda b: (0, 0)),
            pl.BlockSpec((features, wide), lambda b: (0, 0)),
        ],
        out_specs=[
            pl.BlockSpec((copies, slots, 2 * images, features), lambda b: (0, 0, 0, 0)),
            image,
            narrow,
            narrow,
            narrow,
            narrow,
        ],
        out_shape=[
            jax.ShapeDtypeStruct((copies, slots, 2 * images, features), bf16),
            jax.ShapeDtypeStruct((images, tok, features), bf16),
            routing,
            routing,
            routing,
            routing,
        ],
        scratch_shapes=[pltpu.VMEM((wide, features), f32)] * 2,
        compiler_params=pltpu.CompilerParams(vmem_limit_bytes=VMEM),
        cost_estimate=pl.CostEstimate(flops=4 * 10**9, bytes_accessed=14 * 2**20, transcendentals=10**6),
        name="front",
    )(tokens, cotangent, norm_gain, wrep)


gelu_c = 0.7978845608028654
gelu_k = 0.044715


def expert_kernel(act_ref, w_ref, ret_ref, dw_ref, slot_s, cot_s, y_acc, g_acc):
    p = pl.program_id(0)
    peers, rows, features = act_ref.shape
    half = rows // 2
    pair, _, part = w_ref.shape

    @pl.when(p == 0)
    def _():
        act = act_ref[...].astype(f32)
        slot_s[...] = act[:, :half].reshape(peers * half, features).astype(bf16)
        cot_s[...] = act[:, half:].reshape(peers * half, features).astype(bf16)
        y_acc[...] = jnp.zeros_like(y_acc)
        g_acc[...] = jnp.zeros_like(g_acc)

    slots = slot_s[...]
    cots = cot_s[...]
    w1 = jnp.concatenate([w_ref[q, :features] for q in range(pair)], axis=1)
    w2 = jnp.concatenate(
        [
            jnp.concatenate([w_ref[q, pl.ds(features + j * part, part)] for q in range(pair)], axis=0)
            for j in range(features // part)
        ],
        axis=1,
    )
    pre = dot(slots, w1, 1, 0)
    sq = pre * pre
    th = jnp.tanh(gelu_c * (pre + gelu_k * (sq * pre)))
    cdf = 0.5 * (1.0 + th)
    hidden = (pre * cdf).astype(bf16)
    slope = cdf + 0.5 * pre * (1.0 - th * th) * (gelu_c * (1.0 + 3.0 * gelu_k * sq))
    d_act = (dot(cots, w2, 1, 1) * slope).astype(bf16)
    y_acc[...] += dot(hidden, w2, 1, 0)
    g_acc[...] += dot(d_act, w1, 1, 1)
    d_w1 = dot(slots, d_act, 0, 0).astype(bf16)
    d_w2 = dot(hidden, cots, 0, 0).astype(bf16)
    for q in range(pair):
        mine = slice(q * part, (q + 1) * part)
        dw_ref[q, :features] = d_w1[:, mine]
        for j in range(features // part):
            dw_ref[q, pl.ds(features + j * part, part)] = d_w2[mine, j * part : (j + 1) * part]

    @pl.when(p == pl.num_programs(0) - 1)
    def _():
        ret_ref[...] = jnp.concatenate(
            [
                y_acc[...].reshape(peers, half, features),
                g_acc[...].reshape(peers, half, features),
            ],
            axis=1,
        ).astype(bf16)


def expert(act, weights):
    peers, rows, features = act.shape
    parts, long, part = weights.shape
    all_rows = peers * rows // 2
    pair = 2
    whole = pl.BlockSpec((peers, rows, features), lambda p: (0, 0, 0))
    block = pl.BlockSpec((pair, long, part), lambda p: (p, 0, 0))
    return pl.pallas_call(
        expert_kernel,
        grid=(parts // pair,),
        in_specs=[whole, block],
        out_specs=[whole, block],
        out_shape=[
            jax.ShapeDtypeStruct((peers, rows, features), bf16),
            jax.ShapeDtypeStruct((parts, long, part), bf16),
        ],
        scratch_shapes=[
            pltpu.VMEM((all_rows, features), bf16),
            pltpu.VMEM((all_rows, features), bf16),
            pltpu.VMEM((all_rows, features), f32),
            pltpu.VMEM((all_rows, features), f32),
        ],
        compiler_params=pltpu.CompilerParams(vmem_limit_bytes=VMEM),
        cost_estimate=pl.CostEstimate(flops=4 * 10**9, bytes_accessed=10 * 2**20, transcendentals=10**6),
        name="expert",
    )(act, weights)


def back_kernel(
    x_ref, c_ref, normed_ref, pd_ref, pc_ref, lg_ref, st_ref, gain_ref, wrep_t_ref, ret_ref,
    dt_ref, sums_ref, out_s, grad_s, means_s, acc,
):
    b = pl.program_id(0)
    copies, slots, rows, features = ret_ref.shape
    half = rows // 2
    wide = slots * half
    gain = gain_ref[...]

    @pl.when(b == 0)
    def _():
        total = ret_ref[0].astype(f32)
        for copy in range(1, copies):
            total = total + ret_ref[copy].astype(f32)
        out_s[...] = total[:, :half].reshape(wide, features).astype(bf16)
        grad_s[:wide] = total[:, half:].reshape(wide, features).astype(bf16)
        grad_s[wide:] = wrep_t_ref[...]
        means_s[...] = lax.dot_general(
            jnp.broadcast_to(gain, (8, features)),
            grad_s[...].astype(f32),
            (((1,), (1,)), ((), ())),
            preferred_element_type=f32,
            precision=lax.Precision.HIGHEST,
        ) * (1.0 / features)
        acc[...] = jnp.zeros_like(acc)

    normed = normed_ref[0]
    pd = pd_ref[0]
    pc = pc_ref[0]
    d_combine = dot(c_ref[0], out_s[...], 1, 1)
    d_dispatch = dot(normed, grad_s[:wide], 1, 1)
    from_combine = pc * (d_combine - jnp.sum(pc * d_combine, axis=1, keepdims=True))
    from_dispatch = pd * (d_dispatch - jnp.sum(pd * d_dispatch, axis=0, keepdims=True))
    d_logits = (from_combine + from_dispatch).astype(bf16)
    dispatch = pd.astype(bf16)
    coef = jnp.concatenate([dispatch, d_logits], axis=1)
    mean_dot = jnp.sum(
        dispatch.astype(f32) * d_dispatch + d_logits.astype(f32) * lg_ref[0], axis=1, keepdims=True
    ) * (1.0 / features)
    mean_scaled = jnp.sum(coef.astype(f32) * means_s[0:1], axis=1, keepdims=True)
    d_normed = dot(coef, grad_s[...], 1, 0)
    acc[...] += dot(coef, normed, 0, 0)
    mu = st_ref[0, :, 0:1]
    inv = st_ref[0, :, 1:2]
    dt_ref[0] = (
        inv * (d_normed * gain - mean_scaled) - (x_ref[0].astype(f32) - mu) * (inv * inv * mean_dot)
    ).astype(bf16)

    @pl.when(b == pl.num_programs(0) - 1)
    def _():
        d_weight = jnp.sum(acc[wide:].reshape(slots, half, features), axis=1)
        d_gain = jnp.sum(acc[...] * grad_s[...].astype(f32), axis=0, keepdims=True) / gain
        part = sums_ref.shape[2]
        for j in range(features // part):
            cols = slice(j * part, (j + 1) * part)
            sums_ref[j, :slots] = d_weight[:, cols]
            sums_ref[j, slots:] = jnp.broadcast_to(d_gain[:, cols], (8, part))


def back(tokens, cotangent, normed, pd, pc, lg, st, norm_gain, wrep_t, ret, pieces):
    images, tok, features = tokens.shape
    wide = wrep_t.shape[0]
    slots = wide // images
    image = pl.BlockSpec((1, tok, features), lambda b: (b, 0, 0))
    narrow = pl.BlockSpec((1, tok, wide), lambda b: (b, 0, 0))
    sums = (pieces, slots + 8, features // pieces)
    return pl.pallas_call(
        back_kernel,
        grid=(images,),
        in_specs=[
            image,
            image,
            image,
            narrow,
            narrow,
            narrow,
            narrow,
            pl.BlockSpec((1, features), lambda b: (0, 0)),
            pl.BlockSpec((wide, features), lambda b: (0, 0)),
            pl.BlockSpec(ret.shape, lambda b: (0, 0, 0, 0)),
        ],
        out_specs=[image, pl.BlockSpec(sums, lambda b: (0, 0, 0))],
        out_shape=[
            jax.ShapeDtypeStruct((images, tok, features), bf16),
            jax.ShapeDtypeStruct(sums, f32),
        ],
        scratch_shapes=[
            pltpu.VMEM((wide, features), bf16),
            pltpu.VMEM((2 * wide, features), bf16),
            pltpu.VMEM((8, 2 * wide), f32),
            pltpu.VMEM((2 * wide, features), f32),
        ],
        compiler_params=pltpu.CompilerParams(vmem_limit_bytes=VMEM),
        cost_estimate=pl.CostEstimate(flops=6 * 10**9, bytes_accessed=18 * 2**20, transcendentals=0),
        name="back",
    )(tokens, cotangent, normed, pd, pc, lg, st, norm_gain, wrep_t, ret)


def on_device(tokens, norm_gain, slot_weight, w_in, w_out, cotangent):
    images, _, features = tokens.shape
    slots = slot_weight.shape[1]
    part = w_in.shape[2]
    pieces = features // part
    halves = lax.axis_size("yh")
    peers = ("yh", "expert")

    second = w_out[0].reshape(part, pieces, part).swapaxes(0, 1).reshape(features, part)
    weights = lax.all_gather(jnp.concatenate([w_in[0], second], axis=0), "z", axis=0, tiled=False)

    gain = norm_gain[None]
    wrep = jnp.repeat(slot_weight, images, axis=1)
    sent, normed, pd, pc, lg, st = front(tokens, gain, wrep, cotangent, halves)
    act = lax.all_to_all(
        sent.reshape(halves * slots, 2 * images, features), peers, 0, 0, tiled=True
    )
    ret, d_w = expert(act, weights)
    d_w = lax.psum_scatter(d_w, "z", scatter_dimension=0, tiled=False).astype(f32)
    ret = lax.all_to_all(ret, peers, 0, 0, tiled=True)
    d_tokens, sums = back(
        tokens, cotangent, normed, pd, pc, lg, st, gain, wrep.T,
        ret.reshape(halves, slots, 2 * images, features), lax.axis_size("z"),
    )
    sums = jnp.sum(lax.all_to_all(sums, "z", 0, 0, tiled=True), axis=0)
    n_peers = halves * lax.axis_size("expert")
    sums = jnp.sum(
        lax.all_to_all(jnp.broadcast_to(sums[None], (n_peers, *sums.shape)), peers, 0, 0, tiled=True), axis=0
    )
    n_z = lax.axis_size("z")
    sums = lax.all_to_all(jnp.broadcast_to(sums[None], (n_z, *sums.shape)), "z", 0, 0, tiled=True)
    d_slot_weight = sums[:, :slots].swapaxes(1, 2).reshape(features, slots)
    d_gain = sums[:, slots].reshape(features)
    d_first = d_w[:features]
    d_second = d_w[features:].reshape(pieces, part, part).swapaxes(0, 1).reshape(part, features)
    return (d_tokens, d_slot_weight, d_gain, d_first[None], d_second[None])


def solution(mesh):
    dp = mesh.shape["dp"]
    fine = Mesh(mesh.devices.reshape(2, dp // 2, mesh.shape["expert"]), ("yh", "z", "expert"))
    everywhere = P(("yh", "z", "expert"), None, None)
    first = P("expert", None, ("yh", "z"))
    second = P("expert", ("yh", "z"), None)
    return jax.shard_map(
        on_device,
        mesh=fine,
        in_specs=(everywhere, P(), P(), first, second, everywhere),
        out_specs=(everywhere, P(), P(), first, second),
        check_vma=False,
    )
```

```python
import functools

import jax
import jax.numpy as jnp
from jax import lax
from jax.experimental import pallas as pl
from jax.experimental.pallas import tpu as pltpu
from jax.sharding import Mesh
from jax.sharding import PartitionSpec as P

eps = 1e-06
f32 = jnp.float32
bf16 = jnp.bfloat16
VMEM = 60 * 1024 * 1024
RING = 3 * 10**9
RING2 = 3 * 10**9


def dot(a, b, ca, cb):
    return lax.dot_general(a, b, (((ca,), (cb,)), ((), ())), preferred_element_type=f32)


def own(shape, images):
    row = lax.broadcasted_iota(jnp.int32, shape, 0)
    col = lax.broadcasted_iota(jnp.int32, shape, 1)
    return lax.rem(row, images) == lax.rem(col, images)


def replicated(slot_ref, images):
    slots, features = slot_ref.shape
    rows = jnp.broadcast_to(slot_ref[...].astype(f32)[:, None, :], (slots, images, features))
    return rows.reshape(slots * images, features).astype(bf16)


def cuts(rows, shares):
    groups = rows // 16
    at = 0
    out = []
    for k, share in enumerate(shares):
        size = groups - at if k == len(shares) - 1 else groups * share // sum(shares)
        if size:
            out.append(pl.ds(at * 16, size * 16 if k < len(shares) - 1 else rows - at * 16))
        at += size
    return out


def copies_of(src, dst, sem, slices):
    return [pltpu.make_async_copy(src.at[r], dst.at[r], sem.at[k]) for k, r in enumerate(slices)]


def row_softmax(logits, images):
    mine = own(logits.shape, images)
    ec = jnp.where(mine, jnp.exp(logits - jnp.max(logits, axis=1, keepdims=True)), 0.0)
    return ec / jnp.sum(ec, axis=1, keepdims=True)


def front_kernel(
    shares, gain_ref, slot_ref, x_ref, c_ref, out_ref, normed_ref, acc_ref, col_ref,
    x_s, c_s, out_s, normed_s, lg_s, acc_s, x_sem, c_sem, normed_sem, last_sem,
):
    slots, features = slot_ref.shape
    copies, _, images, _ = out_s.shape
    images = images // 2
    slices = cuts(x_s.shape[0], shares)
    x_in = copies_of(x_ref, x_s, x_sem, slices)
    c_in = copies_of(c_ref, c_s, c_sem, slices)
    normed_out = copies_of(normed_s, normed_ref, normed_sem, slices)
    for one, two in zip(x_in, c_in):
        one.start()
        two.start()
    wrep = replicated(slot_ref, images)
    gain = gain_ref[...]
    cot_slots = 0.0
    for k, r in enumerate(slices):
        x_in[k].wait()
        x = x_s[r].astype(f32)
        xc = x - jnp.mean(x, axis=-1, keepdims=True)
        inv = lax.rsqrt(jnp.mean(xc * xc, axis=-1, keepdims=True) + eps)
        normed = (xc * inv * gain).astype(bf16)
        normed_s[r] = normed
        normed_out[k].start()
        logits = dot(normed, wrep, 1, 1)
        lg_s[r] = logits
        pc = row_softmax(logits, images)
        c_in[k].wait()
        cot_slots = cot_slots + dot(pc.astype(bf16), c_s[r], 0, 0)
    lg = lg_s[...]
    lg = jnp.where(own(lg.shape, images), lg, -jnp.inf)
    most = jnp.max(lg, axis=0, keepdims=True)
    ed = jnp.exp(lg - most)
    total = jnp.sum(ed, axis=0, keepdims=True)
    pd = ed / total
    row = lax.broadcasted_iota(jnp.int32, col_ref.shape, 0)
    col_ref[...] = jnp.where(row == 0, most, total)
    got = dot(pd.astype(bf16), normed_s[...], 0, 0)
    both = [got.reshape(slots, images, features), cot_slots.reshape(slots, images, features)]
    both = jnp.concatenate(both, axis=1).astype(bf16)
    for copy in range(copies):
        out_s[copy] = both
    acc_s[...] = got
    last = [
        pltpu.make_async_copy(src, dst, last_sem.at[j])
        for j, (src, dst) in enumerate(((out_s, out_ref), (acc_s, acc_ref)))
    ]
    for copy in last:
        copy.start()
    for copy in normed_out + last:
        copy.wait()


vmem = pl.BlockSpec(memory_space=pltpu.VMEM)
anywhere = pl.BlockSpec(memory_space=pl.ANY)


def front(tokens, norm_gain, slot_t, cotangent, images, copies, shares=(1, 1)):
    rows, features = tokens.shape
    slots = slot_t.shape[0]
    wide = slots * images
    n = len(shares)
    sent = ((copies, slots, 2 * images, features), bf16)
    acc = ((wide, features), f32)
    return pl.pallas_call(
        functools.partial(front_kernel, shares),
        in_specs=[vmem, vmem, anywhere, anywhere],
        out_specs=[anywhere] * 3 + [vmem],
        out_shape=[
            jax.ShapeDtypeStruct(*sent),
            jax.ShapeDtypeStruct((rows, features), bf16),
            jax.ShapeDtypeStruct(*acc),
            jax.ShapeDtypeStruct((8, wide), f32),
        ],
        scratch_shapes=[pltpu.VMEM(tokens.shape, bf16)] * 2
        + [
            pltpu.VMEM(*sent),
            pltpu.VMEM(tokens.shape, bf16),
            pltpu.VMEM((rows, wide), f32),
            pltpu.VMEM(*acc),
            pltpu.SemaphoreType.DMA((n,)),
            pltpu.SemaphoreType.DMA((n,)),
            pltpu.SemaphoreType.DMA((n,)),
            pltpu.SemaphoreType.DMA((2,)),
        ],
        compiler_params=pltpu.CompilerParams(vmem_limit_bytes=VMEM),
        cost_estimate=pl.CostEstimate(flops=8 * 10**9, bytes_accessed=14 * 2**20, transcendentals=10**6),
        name="front",
    )(norm_gain, slot_t, tokens, cotangent)


gelu_c = 0.7978845608028654
gelu_k = 0.044715


def expert_kernel(at_ref, act_ref, *refs):
    n = (len(refs) - 14) // 2
    firsts, seconds = refs[:n], refs[n : 2 * n]
    (
        ret_ref, dw_ref, act_s, w1_s, w2_s, dw_s, ret_s, y_acc, g_acc, act_sem, w1_sem, w2_sem, dw_sem, ret_sem,
    ) = refs[2 * n :]
    peers, rows, features = act_s.shape
    half = rows // 2
    part = seconds[0].shape[0]
    groups = w1_s.shape[0]
    size = n // groups
    act_copy = pltpu.make_async_copy(act_ref, act_s, act_sem)
    act_copy.start()
    copies = []
    for r in range(n):
        g, q = r // size, r % size
        one = pltpu.make_async_copy(firsts[r], w1_s.at[g, :, pl.ds(q * part, part)], w1_sem.at[r])
        two = pltpu.make_async_copy(seconds[r], w2_s.at[g, pl.ds(q * part, part)], w2_sem.at[r])
        one.start()
        two.start()
        copies.append((one, two))
    act_copy.wait()
    act = act_s[...].astype(f32)
    slots = act[:, :half].reshape(peers * half, features).astype(bf16)
    cots = act[:, half:].reshape(peers * half, features).astype(bf16)
    sends = []
    for g in range(groups):
        for q in range(size):
            copies[g * size + q][0].wait()
            copies[g * size + q][1].wait()
        w1 = w1_s[g]
        w2 = w2_s[g]
        pre = dot(slots, w1, 1, 0)
        sq = pre * pre
        th = jnp.tanh(gelu_c * (pre + gelu_k * (sq * pre)))
        cdf = 0.5 * (1.0 + th)
        hidden = (pre * cdf).astype(bf16)
        slope = cdf + 0.5 * pre * (1.0 - th * th) * (gelu_c * (1.0 + 3.0 * gelu_k * sq))
        d_act = (dot(cots, w2, 1, 1) * slope).astype(bf16)
        y = dot(hidden, w2, 1, 0)
        grad = dot(d_act, w1, 1, 1)
        if g:
            y = y + y_acc[...]
            grad = grad + g_acc[...]
        if g < groups - 1:
            y_acc[...] = y
            g_acc[...] = grad
        else:
            ret_s[...] = jnp.concatenate(
                [y.reshape(peers, half, features), grad.reshape(peers, half, features)], axis=1
            ).astype(bf16)
            ret_copy = pltpu.make_async_copy(ret_s, ret_ref, ret_sem)
            ret_copy.start()
        d_w1 = dot(slots, d_act, 0, 0).astype(bf16)
        d_w2 = dot(hidden, cots, 0, 0).astype(bf16)
        for q in range(size):
            r = g * size + q
            mine = slice(q * part, (q + 1) * part)
            dw_s[r, :features] = d_w1[:, mine]
            for j in range(features // part):
                dw_s[r, pl.ds(features + j * part, part)] = d_w2[mine, j * part : (j + 1) * part]
            send = pltpu.make_async_copy(dw_s.at[r], dw_ref.at[lax.rem(at_ref[0] + r, n)], dw_sem.at[r])
            send.start()
            sends.append(send)
    ret_copy.wait()
    for send in sends:
        send.wait()


def expert(at, act, firsts, seconds):
    peers, rows, features = act.shape
    part = firsts[0].shape[1]
    n = len(firsts)
    all_rows = peers * rows // 2
    size = 2
    return pl.pallas_call(
        expert_kernel,
        in_specs=[pl.BlockSpec(memory_space=pltpu.SMEM)] + [anywhere] * (1 + 2 * n),
        out_specs=[anywhere, anywhere],
        out_shape=[
            jax.ShapeDtypeStruct((peers, rows, features), bf16),
            jax.ShapeDtypeStruct((n, 2 * features, part), bf16),
        ],
        scratch_shapes=[
            pltpu.VMEM((peers, rows, features), bf16),
            pltpu.VMEM((n // size, features, size * part), bf16),
            pltpu.VMEM((n // size, size * part, features), bf16),
            pltpu.VMEM((n, 2 * features, part), bf16),
            pltpu.VMEM((peers, rows, features), bf16),
            pltpu.VMEM((all_rows, features), f32),
            pltpu.VMEM((all_rows, features), f32),
            pltpu.SemaphoreType.DMA,
            pltpu.SemaphoreType.DMA((n,)),
            pltpu.SemaphoreType.DMA((n,)),
            pltpu.SemaphoreType.DMA((n,)),
            pltpu.SemaphoreType.DMA,
        ],
        compiler_params=pltpu.CompilerParams(vmem_limit_bytes=VMEM),
        cost_estimate=pl.CostEstimate(flops=4 * 10**9, bytes_accessed=10 * 2**20, transcendentals=10**6),
        name="expert",
    )(at, act, *firsts, *seconds)


def route_kernel(
    shares, gain_ref, slot_ref, col_ref, c_ref, normed_ref, ret_ref, acc_ref,
    sums_ref, coef_ref, grad_ref,
    c_s, normed_s, ret_s, acc_s, coef_s, grad_s, out_s, pd_s, dd_s, fc_s,
    c_sem, normed_sem, whole_sem, coef_sem,
):
    copies, slots, images, features = ret_s.shape
    images = images // 2
    wide = slots * images
    slices = cuts(c_s.shape[0], shares)
    c_in = copies_of(c_ref, c_s, c_sem, slices)
    normed_in = copies_of(normed_ref, normed_s, normed_sem, slices)
    coef_out = copies_of(coef_s, coef_ref, coef_sem, slices)
    ret_in = pltpu.make_async_copy(ret_ref, ret_s, whole_sem.at[0])
    acc_in = pltpu.make_async_copy(acc_ref, acc_s, whole_sem.at[1])
    grad_out = pltpu.make_async_copy(grad_s, grad_ref, whole_sem.at[2])
    normed_in[0].start()
    ret_in.start()
    c_in[0].start()
    for k in range(1, len(slices)):
        normed_in[k].start()
        c_in[k].start()
    acc_in.start()
    wrep = replicated(slot_ref, images)
    grad_s[wide:] = wrep
    most, total = col_ref[0:1], col_ref[1:2]
    ret_in.wait()
    got = ret_s[0].astype(f32)
    for copy in range(1, copies):
        got = got + ret_s[copy].astype(f32)
    out_s[...] = got[:, :images].reshape(wide, features).astype(bf16)
    grad_s[:wide] = got[:, images:].reshape(wide, features).astype(bf16)
    grad_out.start()
    col_sum = jnp.zeros((1, wide), f32)
    for k, r in enumerate(slices):
        normed_in[k].wait()
        logits = dot(normed_s[r], wrep, 1, 1)
        pc = row_softmax(logits, images)
        pd = jnp.where(own(logits.shape, images), jnp.exp(logits - most) / total, 0.0)
        dd = dot(normed_s[r], grad_s[:wide], 1, 1)
        c_in[k].wait()
        d_combine = dot(c_s[r], out_s[...], 1, 1)
        fc_s[r] = pc * (d_combine - jnp.sum(pc * d_combine, axis=1, keepdims=True))
        pd_s[r] = pd
        dd_s[r] = dd
        col_sum = col_sum + jnp.sum(pd * dd, axis=0, keepdims=True)
    for k, r in enumerate(slices):
        pd = pd_s[r]
        coef_s[r, :wide] = pd.astype(bf16)
        coef_s[r, wide:] = (fc_s[r] + pd * (dd_s[r] - col_sum)).astype(bf16)
        coef_out[k].start()
    acc = dot(coef_s[:, wide:], normed_s[...], 0, 0)
    acc_in.wait()
    d_weight = jnp.sum(acc.reshape(slots, images, features), axis=1)
    d_gain = jnp.sum(acc_s[...] * grad_s[:wide].astype(f32), axis=0, keepdims=True)
    d_gain = d_gain + jnp.sum(acc * grad_s[wide:].astype(f32), axis=0, keepdims=True)
    d_gain = d_gain / gain_ref[...]
    pieces, _, part = sums_ref.shape
    blocks = features // part // pieces
    for k in range(pieces):
        start = k * blocks * part
        for j in range(blocks):
            sums_ref[k, j * slots : (j + 1) * slots] = d_weight[:, start + j * part : start + (j + 1) * part]
        last = [d_gain[:, start + j * part : start + (j + 1) * part] for j in range(blocks)]
        last.append(jnp.zeros((8 - blocks, part), f32))
        sums_ref[k, blocks * slots :] = jnp.concatenate(last, axis=0)
    for copy in coef_out:
        copy.wait()
    grad_out.wait()


def route(cotangent, normed, norm_gain, slot_t, col, ret, acc, pieces, shares=(1, 1)):
    rows, features = cotangent.shape
    _, slots, images, _ = ret.shape
    wide = slots * images // 2
    n = len(shares)
    ins = (cotangent, normed, ret, acc)
    outs = [((rows, 2 * wide), bf16), ((2 * wide, features), bf16)]
    sums = jax.ShapeDtypeStruct((pieces, features // 128 // pieces * slots + 8, 128), f32)
    return pl.pallas_call(
        functools.partial(route_kernel, shares),
        in_specs=[vmem] * 3 + [anywhere] * len(ins),
        out_specs=[vmem] + [anywhere] * len(outs),
        out_shape=[sums] + [jax.ShapeDtypeStruct(*out) for out in outs],
        scratch_shapes=[pltpu.VMEM(x.shape, x.dtype) for x in ins]
        + [pltpu.VMEM(*out) for out in outs]
        + [
            pltpu.VMEM((wide, features), bf16),
            pltpu.VMEM((rows, wide), f32),
            pltpu.VMEM((rows, wide), f32),
            pltpu.VMEM((rows, wide), f32),
            pltpu.SemaphoreType.DMA((n,)),
            pltpu.SemaphoreType.DMA((n,)),
            pltpu.SemaphoreType.DMA((3,)),
            pltpu.SemaphoreType.DMA((n,)),
        ],
        compiler_params=pltpu.CompilerParams(vmem_limit_bytes=VMEM),
        cost_estimate=pl.CostEstimate(flops=5 * 10**9, bytes_accessed=14 * 2**20, transcendentals=0),
        name="route",
    )(norm_gain, slot_t, col, *ins)


def back_kernel(gain_ref, grad_ref, x_ref, coef_ref, dt_ref):
    x = x_ref[...].astype(f32)
    xc = x - jnp.mean(x, axis=-1, keepdims=True)
    inv = lax.rsqrt(jnp.mean(xc * xc, axis=-1, keepdims=True) + eps)
    x_hat = xc * inv
    scaled = dot(coef_ref[...], grad_ref[...], 1, 0) * gain_ref[...]
    mean_scaled = jnp.mean(scaled, axis=-1, keepdims=True)
    mean_dot = jnp.mean(scaled * x_hat, axis=-1, keepdims=True)
    dt_ref[...] = (inv * (scaled - mean_scaled - x_hat * mean_dot)).astype(bf16)


def back(tokens, coef, norm_gain, grad):
    rows, features = tokens.shape
    wide = coef.shape[1]
    steps = 2 if rows % 32 == 0 else 1
    block = pl.BlockSpec((rows // steps, features), lambda i: (i, 0))
    return pl.pallas_call(
        back_kernel,
        grid=(steps,),
        in_specs=[
            pl.BlockSpec((1, features), lambda i: (0, 0)),
            pl.BlockSpec((wide, features), lambda i: (0, 0)),
            block,
            pl.BlockSpec((rows // steps, wide), lambda i: (i, 0)),
        ],
        out_specs=block,
        out_shape=jax.ShapeDtypeStruct(tokens.shape, bf16),
        compiler_params=pltpu.CompilerParams(vmem_limit_bytes=VMEM),
        cost_estimate=pl.CostEstimate(flops=5 * 10**9, bytes_accessed=8 * 2**20, transcendentals=0),
        name="back",
    )(norm_gain, grad, tokens, coef)


def gate_kernel(*refs):
    pass


def after(kept, others, weight=0):
    return pl.pallas_call(
        gate_kernel,
        in_specs=[anywhere] * (len(kept) + len(others)),
        out_specs=[anywhere] * len(kept),
        out_shape=[jax.ShapeDtypeStruct(x.shape, x.dtype) for x in kept],
        input_output_aliases={i: i for i in range(len(kept))},
        cost_estimate=pl.CostEstimate(flops=weight, bytes_accessed=0, transcendentals=0),
        name="after",
    )(*kept, *others)


def on_device(tokens, norm_gain, slot_weight, w_in, w_out, cotangent):
    images, _, features = tokens.shape
    slots = slot_weight.shape[1]
    part = w_in.shape[2]
    halves = lax.axis_size("yh")
    peers = ("yh", "yl", "x", "c")

    n = lax.axis_size("z")
    up = [(i, (i + 1) % n) for i in range(n)]
    down = [(i, (i - 1) % n) for i in range(n)]
    firsts = {0: w_in[0]}
    seconds = {0: w_out[0]}

    def step(k):
        firsts[n - k] = lax.ppermute(firsts[(n - k + 1) % n], "z", up)
        seconds[k] = lax.ppermute(seconds[k - 1], "z", down)
        if k < n - k:
            firsts[k] = lax.ppermute(firsts[k - 1], "z", down)
            seconds[n - k] = lax.ppermute(seconds[(n - k + 1) % n], "z", up)

    step(1)
    gain = norm_gain[None]
    slot_t = slot_weight.T
    tok = tokens.shape[1]
    by_place = tokens.swapaxes(0, 1).reshape(tok * images, features)
    cots = cotangent.swapaxes(0, 1).reshape(tok * images, features)
    sent, normed, acc, col = front(by_place, gain, slot_t, cots, images, halves)
    sent, firsts[1], firsts[n - 1], seconds[1], seconds[n - 1] = after(
        [sent, firsts[1], firsts[n - 1], seconds[1], seconds[n - 1]], []
    )
    act = lax.all_to_all(
        sent.reshape(halves * slots, 2 * images, features), peers, 0, 0, tiled=True
    )
    for k in range(2, n // 2 + 1):
        step(k)
    far = n // 2
    firsts[far], seconds[far] = after([firsts[far], seconds[far]], [], RING)
    if n > 3:
        firsts[far - 1], seconds[far + 1] = after([firsts[far - 1], seconds[far + 1]], [], RING2)
    at = lax.axis_index("z").reshape(1)
    ret, d_w = expert(at, act, [firsts[r] for r in range(n)], [seconds[r] for r in range(n)])
    d_w = lax.psum_scatter(d_w, "z", scatter_dimension=0, tiled=False).astype(f32)
    ret = lax.all_to_all(ret, peers, 0, 0, tiled=True)
    cores = lax.axis_size("c")
    ret = ret.reshape(halves, slots, 2 * images, features)
    sums, coef, grad = route(cots, normed, gain, slot_t, col, ret, acc, cores)

    core = lax.axis_index("c")
    swap = [(0, 1), (1, 0)]
    other = lax.ppermute(lax.dynamic_index_in_dim(sums, 1 - core, 0, False), "c", swap)
    share = lax.dynamic_index_in_dim(sums, core, 0, False) + other

    def total(share, axes, others=()):
        many = 1
        for axis in axes:
            many *= lax.axis_size(axis)
        copies = jnp.broadcast_to(share[None], (many, *share.shape))
        (copies,) = after([lax.all_to_all(copies, axes, 0, 0, tiled=True)], others)
        return jnp.sum(copies, axis=0)

    d_tokens = back(by_place, coef, gain, grad)
    share = total(share, ("yh", "yl", "x"), [d_tokens])
    pieces = features // part
    d_first = d_w[:features]
    d_second = d_w[features:].reshape(pieces, part, part).swapaxes(0, 1).reshape(part, features)
    share = total(share, ("z",), [d_first, d_second])
    other = lax.ppermute(share, "c", swap)
    sums = jnp.stack([jnp.where(core == 0, share, other), jnp.where(core == 0, other, share)])
    blocks = features // sums.shape[2] // cores
    d_slot_weight = sums[:, : blocks * slots].reshape(cores * blocks, slots, -1)
    d_slot_weight = d_slot_weight.swapaxes(0, 1).reshape(slots, features).T
    d_gain = sums[:, blocks * slots : blocks * slots + blocks].reshape(features)
    d_tokens = d_tokens.reshape(tok, images, features).swapaxes(0, 1)
    return (d_tokens, d_slot_weight, d_gain, d_first[None], d_second[None])


def solution(mesh):
    fine = Mesh(
        mesh.devices.reshape(2, mesh.shape["dp"] // 2, 2, mesh.shape["expert"] // 4, 2),
        ("yh", "z", "yl", "x", "c"),
    )
    everywhere = P(("yh", "z", "yl", "x", "c"), None, None)
    first = P(("yl", "x", "c"), None, ("yh", "z"))
    second = P(("yl", "x", "c"), ("yh", "z"), None)
    return jax.shard_map(
        on_device,
        mesh=fine,
        in_specs=(everywhere, P(), P(), first, second, everywhere),
        out_specs=(everywhere, P(), P(), first, second),
        check_vma=False,
    )
```

```python
import functools

import jax
import jax.numpy as jnp
from jax import lax
from jax.experimental import pallas as pl
from jax.experimental.pallas import tpu as pltpu
from jax.sharding import Mesh
from jax.sharding import PartitionSpec as P

eps = 1e-06
f32 = jnp.float32
bf16 = jnp.bfloat16
VMEM = 60 * 1024 * 1024
RING = 3 * 10**9
RING2 = 3 * 10**9
LOW = 1024 * 1024


def dot(a, b, ca, cb):
    return lax.dot_general(a, b, (((ca,), (cb,)), ((), ())), preferred_element_type=f32)


def own(shape, images):
    row = lax.broadcasted_iota(jnp.int32, shape, 0)
    col = lax.broadcasted_iota(jnp.int32, shape, 1)
    return lax.rem(row, images) == lax.rem(col, images)


def replicated(slot_ref, images):
    slots, features = slot_ref.shape
    rows = jnp.broadcast_to(slot_ref[...].astype(f32)[:, None, :], (slots, images, features))
    return rows.reshape(slots * images, features).astype(bf16)


def cuts(rows, shares):
    groups = rows // 16
    at = 0
    out = []
    for k, share in enumerate(shares):
        size = groups - at if k == len(shares) - 1 else groups * share // sum(shares)
        if size:
            out.append(pl.ds(at * 16, size * 16 if k < len(shares) - 1 else rows - at * 16))
        at += size
    return out


def copies_of(src, dst, sem, slices):
    return [pltpu.make_async_copy(src.at[r], dst.at[r], sem.at[k]) for k, r in enumerate(slices)]


def row_softmax(logits, images):
    mine = own(logits.shape, images)
    ec = jnp.where(mine, jnp.exp(logits - jnp.max(logits, axis=1, keepdims=True)), 0.0)
    return ec / jnp.sum(ec, axis=1, keepdims=True)


def front_kernel(
    shares, gain_ref, slot_ref, x_ref, c_ref, out_ref, normed_ref, acc_ref, col_ref,
    x_s, c_s, out_s, normed_s, lg_s, acc_s, x_sem, c_sem, normed_sem, last_sem,
):
    slots, features = slot_ref.shape
    copies, _, images, _ = out_s.shape
    images = images // 2
    slices = cuts(x_s.shape[0], shares)
    x_in = copies_of(x_ref, x_s, x_sem, slices)
    c_in = copies_of(c_ref, c_s, c_sem, slices)
    normed_out = copies_of(normed_s, normed_ref, normed_sem, slices)
    for one, two in zip(x_in, c_in):
        one.start()
        two.start()
    wrep = replicated(slot_ref, images)
    gain = gain_ref[...]
    cot_slots = 0.0
    for k, r in enumerate(slices):
        x_in[k].wait()
        x = x_s[r].astype(f32)
        xc = x - jnp.mean(x, axis=-1, keepdims=True)
        inv = lax.rsqrt(jnp.mean(xc * xc, axis=-1, keepdims=True) + eps)
        normed = (xc * inv * gain).astype(bf16)
        normed_s[r] = normed
        normed_out[k].start()
        logits = dot(normed, wrep, 1, 1)
        lg_s[r] = logits
        pc = row_softmax(logits, images)
        c_in[k].wait()
        cot_slots = cot_slots + dot(pc.astype(bf16), c_s[r], 0, 0)
    lg = lg_s[...]
    lg = jnp.where(own(lg.shape, images), lg, -jnp.inf)
    most = jnp.max(lg, axis=0, keepdims=True)
    ed = jnp.exp(lg - most)
    total = jnp.sum(ed, axis=0, keepdims=True)
    pd = ed / total
    row = lax.broadcasted_iota(jnp.int32, col_ref.shape, 0)
    col_ref[...] = jnp.where(row == 0, most, total)
    got = dot(pd.astype(bf16), normed_s[...], 0, 0)
    both = [got.reshape(slots, images, features), cot_slots.reshape(slots, images, features)]
    both = jnp.concatenate(both, axis=1).astype(bf16)
    for copy in range(copies):
        out_s[copy] = both
    acc_s[...] = got
    last = [
        pltpu.make_async_copy(src, dst, last_sem.at[j])
        for j, (src, dst) in enumerate(((out_s, out_ref), (acc_s, acc_ref)))
    ]
    for copy in last:
        copy.start()
    for copy in normed_out + last:
        copy.wait()


vmem = pl.BlockSpec(memory_space=pltpu.VMEM)
anywhere = pl.BlockSpec(memory_space=pl.ANY)


def front(tokens, norm_gain, slot_t, cotangent, images, copies, shares=(1, 1)):
    rows, features = tokens.shape
    slots = slot_t.shape[0]
    wide = slots * images
    n = len(shares)
    sent = ((copies, slots, 2 * images, features), bf16)
    acc = ((wide, features), f32)
    return pl.pallas_call(
        functools.partial(front_kernel, shares),
        in_specs=[vmem, vmem, anywhere, anywhere],
        out_specs=[anywhere] * 3 + [vmem],
        out_shape=[
            jax.ShapeDtypeStruct(*sent),
            jax.ShapeDtypeStruct((rows, features), bf16),
            jax.ShapeDtypeStruct(*acc),
            jax.ShapeDtypeStruct((8, wide), f32),
        ],
        scratch_shapes=[pltpu.VMEM(tokens.shape, bf16)] * 2
        + [
            pltpu.VMEM(*sent),
            pltpu.VMEM(tokens.shape, bf16),
            pltpu.VMEM((rows, wide), f32),
            pltpu.VMEM(*acc),
            pltpu.SemaphoreType.DMA((n,)),
            pltpu.SemaphoreType.DMA((n,)),
            pltpu.SemaphoreType.DMA((n,)),
            pltpu.SemaphoreType.DMA((2,)),
        ],
        compiler_params=pltpu.CompilerParams(vmem_limit_bytes=VMEM),
        cost_estimate=pl.CostEstimate(flops=8 * 10**9, bytes_accessed=14 * 2**20, transcendentals=10**6),
        name="front",
    )(norm_gain, slot_t, tokens, cotangent)


gelu_c = 0.7978845608028654
gelu_k = 0.044715


def expert_kernel(n, act_ref, *refs):
    firsts, seconds = refs[:n], refs[n : 2 * n]
    ret_ref, dw_refs = refs[2 * n], refs[2 * n + 1 : 3 * n + 1]
    (
        act_s, w1_s, w2_s, dw_s, ret_s, y_acc, g_acc, act_sem, w1_sem, w2_sem, dw_sem, ret_sem,
    ) = refs[3 * n + 1 :]
    peers, rows, features = act_s.shape
    half = rows // 2
    part = seconds[0].shape[0]
    groups = w1_s.shape[0]
    size = n // groups
    act_copy = pltpu.make_async_copy(act_ref, act_s, act_sem)
    act_copy.start()
    copies = []
    for r in range(n):
        g, q = r // size, r % size
        one = pltpu.make_async_copy(firsts[r], w1_s.at[g, :, pl.ds(q * part, part)], w1_sem.at[r])
        two = pltpu.make_async_copy(seconds[r], w2_s.at[g, pl.ds(q * part, part)], w2_sem.at[r])
        one.start()
        two.start()
        copies.append((one, two))
    act_copy.wait()
    act = act_s[...].astype(f32)
    slots = act[:, :half].reshape(peers * half, features).astype(bf16)
    cots = act[:, half:].reshape(peers * half, features).astype(bf16)
    sends = []
    for g in range(groups):
        for q in range(size):
            copies[g * size + q][0].wait()
            copies[g * size + q][1].wait()
        w1 = w1_s[g]
        w2 = w2_s[g]
        pre = dot(slots, w1, 1, 0)
        sq = pre * pre
        th = jnp.tanh(gelu_c * (pre + gelu_k * (sq * pre)))
        cdf = 0.5 * (1.0 + th)
        hidden = (pre * cdf).astype(bf16)
        slope = cdf + 0.5 * pre * (1.0 - th * th) * (gelu_c * (1.0 + 3.0 * gelu_k * sq))
        d_act = (dot(cots, w2, 1, 1) * slope).astype(bf16)
        y = dot(hidden, w2, 1, 0)
        grad = dot(d_act, w1, 1, 1)
        if g:
            y = y + y_acc[...]
            grad = grad + g_acc[...]
        if g < groups - 1:
            y_acc[...] = y
            g_acc[...] = grad
        else:
            ret_s[...] = jnp.concatenate(
                [y.reshape(peers, half, features), grad.reshape(peers, half, features)], axis=1
            ).astype(bf16)
            ret_copy = pltpu.make_async_copy(ret_s, ret_ref, ret_sem)
            ret_copy.start()
        d_w1 = dot(slots, d_act, 0, 0).astype(bf16)
        d_w2 = dot(hidden, cots, 0, 0).astype(bf16)
        for q in range(size):
            r = g * size + q
            mine = slice(q * part, (q + 1) * part)
            dw_s[r, :features] = d_w1[:, mine]
            for j in range(features // part):
                dw_s[r, pl.ds(features + j * part, part)] = d_w2[mine, j * part : (j + 1) * part]
            send = pltpu.make_async_copy(dw_s.at[r], dw_refs[r], dw_sem.at[r])
            send.start()
            sends.append(send)
    ret_copy.wait()
    for send in sends:
        send.wait()


def expert(act, firsts, seconds):
    peers, rows, features = act.shape
    part = firsts[0].shape[1]
    n = len(firsts)
    all_rows = peers * rows // 2
    size = 4 if n % 4 == 0 else 1
    wide = pltpu.VMEM((n // size, features, size * part), bf16)
    tall = pltpu.VMEM((n // size, size * part, features), bf16)
    got = pl.pallas_call(
        functools.partial(expert_kernel, n),
        in_specs=[anywhere] * (1 + 2 * n),
        out_specs=[anywhere] * (1 + n),
        out_shape=[jax.ShapeDtypeStruct(act.shape, bf16)]
        + [jax.ShapeDtypeStruct((2 * features, part), bf16)] * n,
        scratch_shapes=[
            pltpu.VMEM((peers, rows, features), bf16),
            wide,
            tall,
            pltpu.VMEM((n, 2 * features, part), bf16),
            pltpu.VMEM((peers, rows, features), bf16),
            pltpu.VMEM((all_rows, features), f32),
            pltpu.VMEM((all_rows, features), f32),
            pltpu.SemaphoreType.DMA,
            pltpu.SemaphoreType.DMA((n,)),
            pltpu.SemaphoreType.DMA((n,)),
            pltpu.SemaphoreType.DMA((n,)),
            pltpu.SemaphoreType.DMA,
        ],
        compiler_params=pltpu.CompilerParams(vmem_limit_bytes=VMEM),
        cost_estimate=pl.CostEstimate(flops=4 * 10**9, bytes_accessed=10 * 2**20, transcendentals=10**6),
        name="expert",
    )(act, *firsts, *seconds)
    return got[0], got[1:]


def add_up_kernel(*refs):
    total = 0.0
    for ref in refs[:-1]:
        for k in range(ref.shape[0]):
            total = total + ref[k]
    for k in range(refs[-1].shape[0]):
        refs[-1][k] = total


def add_up(arrays, copies):
    return pl.pallas_call(
        add_up_kernel,
        in_specs=[vmem] * len(arrays),
        out_specs=vmem,
        out_shape=jax.ShapeDtypeStruct((copies, *arrays[0].shape[1:]), f32),
        compiler_params=pltpu.CompilerParams(vmem_limit_bytes=8 * 1024 * 1024),
        cost_estimate=pl.CostEstimate(flops=10**8, bytes_accessed=2**20, transcendentals=0),
        name="add_up",
    )(*arrays)


def route_kernel(
    shares, core_ref, gain_ref, slot_ref, col_ref, c_ref, normed_ref, ret_ref, acc_ref,
    mine_ref, other_ref, coef_ref, grad_ref,
    c_s, normed_s, ret_s, acc_s, coef_s, grad_s, out_s, pd_s, dd_s, fc_s,
    c_sem, normed_sem, whole_sem, coef_sem,
):
    copies, slots, images, features = ret_s.shape
    images = images // 2
    wide = slots * images
    slices = cuts(c_s.shape[0], shares)
    c_in = copies_of(c_ref, c_s, c_sem, slices)
    normed_in = copies_of(normed_ref, normed_s, normed_sem, slices)
    coef_out = copies_of(coef_s, coef_ref, coef_sem, slices)
    ret_in = pltpu.make_async_copy(ret_ref, ret_s, whole_sem.at[0])
    acc_in = pltpu.make_async_copy(acc_ref, acc_s, whole_sem.at[1])
    grad_out = pltpu.make_async_copy(grad_s, grad_ref, whole_sem.at[2])
    ret_in.start()
    for one, two in zip(normed_in, c_in):
        one.start()
        two.start()
    acc_in.start()
    wrep = replicated(slot_ref, images)
    grad_s[wide:] = wrep
    most, total = col_ref[0:1], col_ref[1:2]
    ret_in.wait()
    got = ret_s[0].astype(f32)
    for copy in range(1, copies):
        got = got + ret_s[copy].astype(f32)
    out_s[...] = got[:, :images].reshape(wide, features).astype(bf16)
    grad_s[:wide] = got[:, images:].reshape(wide, features).astype(bf16)
    grad_out.start()
    col_sum = jnp.zeros((1, wide), f32)
    for k, r in enumerate(slices):
        normed_in[k].wait()
        logits = dot(normed_s[r], wrep, 1, 1)
        pc = row_softmax(logits, images)
        pd = jnp.where(own(logits.shape, images), jnp.exp(logits - most) / total, 0.0)
        dd = dot(normed_s[r], grad_s[:wide], 1, 1)
        c_in[k].wait()
        d_combine = dot(c_s[r], out_s[...], 1, 1)
        fc_s[r] = pc * (d_combine - jnp.sum(pc * d_combine, axis=1, keepdims=True))
        pd_s[r] = pd
        dd_s[r] = dd
        col_sum = col_sum + jnp.sum(pd * dd, axis=0, keepdims=True)
    for k, r in enumerate(slices):
        pd = pd_s[r]
        coef_s[r, :wide] = pd.astype(bf16)
        coef_s[r, wide:] = (fc_s[r] + pd * (dd_s[r] - col_sum)).astype(bf16)
        coef_out[k].start()
    acc = dot(coef_s[:, wide:], normed_s[...], 0, 0)
    acc_in.wait()
    d_weight = jnp.sum(acc.reshape(slots, images, features), axis=1)
    d_gain = jnp.sum(acc_s[...] * grad_s[:wide].astype(f32), axis=0, keepdims=True)
    d_gain = d_gain + jnp.sum(acc * grad_s[wide:].astype(f32), axis=0, keepdims=True)
    d_gain = d_gain / gain_ref[...]
    part = mine_ref.shape[1]
    blocks = features // part // 2
    first = core_ref[0] == 0

    def chosen(j, rows):
        low = rows[:, j * part : (j + 1) * part]
        high = rows[:, (blocks + j) * part : (blocks + j + 1) * part]
        return jnp.where(first, low, high), jnp.where(first, high, low)

    for j in range(blocks):
        here = slice(j * slots, (j + 1) * slots)
        mine_ref[here], other_ref[here] = chosen(j, d_weight)
    last = [chosen(j, d_gain) for j in range(blocks)]
    rest = jnp.zeros((8 - blocks, part), f32)
    mine_ref[blocks * slots :] = jnp.concatenate([one for one, _ in last] + [rest], axis=0)
    other_ref[blocks * slots :] = jnp.concatenate([two for _, two in last] + [rest], axis=0)
    for copy in coef_out:
        copy.wait()
    grad_out.wait()


def route(core, cotangent, normed, norm_gain, slot_t, col, ret, acc, shares=(1, 1)):
    rows, features = cotangent.shape
    _, slots, images, _ = ret.shape
    wide = slots * images // 2
    n = len(shares)
    ins = (cotangent, normed, ret, acc)
    outs = [((rows, 2 * wide), bf16), ((2 * wide, features), bf16)]
    sums = jax.ShapeDtypeStruct((features // 256 * slots + 8, 128), f32)
    return pl.pallas_call(
        functools.partial(route_kernel, shares),
        in_specs=[pl.BlockSpec(memory_space=pltpu.SMEM)] + [vmem] * 3 + [anywhere] * len(ins),
        out_specs=[vmem] * 2 + [anywhere] * len(outs),
        out_shape=[sums] * 2 + [jax.ShapeDtypeStruct(*out) for out in outs],
        scratch_shapes=[pltpu.VMEM(x.shape, x.dtype) for x in ins]
        + [pltpu.VMEM(*out) for out in outs]
        + [
            pltpu.VMEM((wide, features), bf16),
            pltpu.VMEM((rows, wide), f32),
            pltpu.VMEM((rows, wide), f32),
            pltpu.VMEM((rows, wide), f32),
            pltpu.SemaphoreType.DMA((n,)),
            pltpu.SemaphoreType.DMA((n,)),
            pltpu.SemaphoreType.DMA((3,)),
            pltpu.SemaphoreType.DMA((n,)),
        ],
        compiler_params=pltpu.CompilerParams(vmem_limit_bytes=VMEM),
        cost_estimate=pl.CostEstimate(flops=5 * 10**9, bytes_accessed=14 * 2**20, transcendentals=0),
        name="route",
    )(core, norm_gain, slot_t, col, *ins)


def back_kernel(gain_ref, grad_ref, x_ref, coef_ref, dt_ref):
    x = x_ref[...].astype(f32)
    xc = x - jnp.mean(x, axis=-1, keepdims=True)
    inv = lax.rsqrt(jnp.mean(xc * xc, axis=-1, keepdims=True) + eps)
    x_hat = xc * inv
    scaled = dot(coef_ref[...], grad_ref[...], 1, 0) * gain_ref[...]
    mean_scaled = jnp.mean(scaled, axis=-1, keepdims=True)
    mean_dot = jnp.mean(scaled * x_hat, axis=-1, keepdims=True)
    dt_ref[...] = (inv * (scaled - mean_scaled - x_hat * mean_dot)).astype(bf16)


def back(tokens, coef, norm_gain, grad):
    rows, features = tokens.shape
    wide = coef.shape[1]
    steps = 2 if rows % 32 == 0 else 1
    block = pl.BlockSpec((rows // steps, features), lambda i: (i, 0))
    return pl.pallas_call(
        back_kernel,
        grid=(steps,),
        in_specs=[
            pl.BlockSpec((1, features), lambda i: (0, 0)),
            pl.BlockSpec((wide, features), lambda i: (0, 0)),
            block,
            pl.BlockSpec((rows // steps, wide), lambda i: (i, 0)),
        ],
        out_specs=block,
        out_shape=jax.ShapeDtypeStruct(tokens.shape, bf16),
        compiler_params=pltpu.CompilerParams(vmem_limit_bytes=VMEM),
        cost_estimate=pl.CostEstimate(flops=5 * 10**9, bytes_accessed=8 * 2**20, transcendentals=0),
        name="back",
    )(norm_gain, grad, tokens, coef)


def gate_kernel(*refs):
    pass


def after(kept, others, weight=0, limit=None):
    return pl.pallas_call(
        gate_kernel,
        in_specs=[anywhere] * (len(kept) + len(others)),
        out_specs=[anywhere] * len(kept),
        out_shape=[jax.ShapeDtypeStruct(x.shape, x.dtype) for x in kept],
        input_output_aliases={i: i for i in range(len(kept))},
        compiler_params=pltpu.CompilerParams(vmem_limit_bytes=limit),
        cost_estimate=pl.CostEstimate(flops=weight, bytes_accessed=0, transcendentals=0),
        name="after",
    )(*kept, *others)


def on_device(tokens, norm_gain, slot_weight, w_in, w_out, cotangent):
    images, _, features = tokens.shape
    slots = slot_weight.shape[1]
    part = w_in.shape[2]
    halves = lax.axis_size("yh")
    peers = ("yh", "yl", "x", "c")

    n = lax.axis_size("z")
    up = [(i, (i + 1) % n) for i in range(n)]
    down = [(i, (i - 1) % n) for i in range(n)]
    firsts = {0: w_in[0]}
    seconds = {0: w_out[0]}

    def step(k):
        firsts[n - k] = lax.ppermute(firsts[(n - k + 1) % n], "z", up)
        seconds[k] = lax.ppermute(seconds[k - 1], "z", down)
        if k < n - k:
            firsts[k] = lax.ppermute(firsts[k - 1], "z", down)
            seconds[n - k] = lax.ppermute(seconds[(n - k + 1) % n], "z", up)

    step(1)
    gain = norm_gain[None]
    slot_t = slot_weight.T
    tok = tokens.shape[1]
    by_place = tokens.swapaxes(0, 1).reshape(tok * images, features)
    cots = cotangent.swapaxes(0, 1).reshape(tok * images, features)
    sent, normed, acc, col = front(by_place, gain, slot_t, cots, images, halves)
    sent, firsts[1], firsts[n - 1], seconds[1], seconds[n - 1] = after(
        [sent, firsts[1], firsts[n - 1], seconds[1], seconds[n - 1]], []
    )
    act = lax.all_to_all(
        sent.reshape(halves * slots, 2 * images, features), peers, 0, 0, tiled=True
    )
    for k in range(2, n // 2 + 1):
        step(k)
    far = n // 2
    firsts[far], seconds[far] = after([firsts[far], seconds[far]], [], RING)
    if n > 3:
        firsts[far - 1], seconds[far + 1] = after([firsts[far - 1], seconds[far + 1]], [], RING2)
    ret, d_w = expert(act, [firsts[r] for r in range(n)], [seconds[r] for r in range(n)])
    ret = lax.all_to_all(ret, peers, 0, 0, tiled=True)

    state = [d_w[far], d_w[(far + 1) % n]]

    def pass_on(k):
        state[0] = lax.ppermute(state[0], "z", up)
        if k < far:
            state[1] = lax.ppermute(state[1], "z", down)

    def add_own(k):
        state[0] = state[0] + d_w[far - k]
        if k < far - 1:
            state[1] = state[1] + d_w[far + 1 + k]

    pass_on(1)
    if far > 2:
        add_own(1)
        pass_on(2)
    done = 2 if far > 2 else 1

    core = lax.axis_index("c")
    swap = [(0, 1), (1, 0)]
    ret = ret.reshape(halves, slots, 2 * images, features)
    mine, other, coef, grad = route(core.reshape(1), cots, normed, gain, slot_t, col, ret, acc)
    plane = ("yh", "yl", "x")
    n_plane = halves * lax.axis_size("yl") * lax.axis_size("x")
    copies = add_up([mine[None], lax.ppermute(other, "c", swap)[None]], n_plane)
    state = list(after(state, [copies], limit=LOW))
    copies = lax.all_to_all(copies, plane, 0, 0, tiled=True)
    for k in range(done, far):
        add_own(k)
        pass_on(k + 1)
    copies = add_up([copies], n)
    (late_gain,) = after([gain], [copies], limit=LOW)
    d_tokens = back(by_place, coef, late_gain, grad)
    (share,) = add_up([lax.all_to_all(copies, "z", 0, 0, tiled=True)], 1)
    pieces = features // part
    total = (d_w[0].astype(f32) + state[0].astype(f32)) + state[1].astype(f32)
    d_first = total[:features]
    d_second = total[features:].reshape(pieces, part, part).swapaxes(0, 1).reshape(part, features)
    other = lax.ppermute(share, "c", swap)
    sums = jnp.stack([jnp.where(core == 0, share, other), jnp.where(core == 0, other, share)])
    blocks = features // sums.shape[2] // 2
    d_slot_weight = sums[:, : blocks * slots].reshape(2 * blocks, slots, -1)
    d_slot_weight = d_slot_weight.swapaxes(0, 1).reshape(slots, features).T
    d_gain = sums[:, blocks * slots : blocks * slots + blocks].reshape(features)
    d_tokens = d_tokens.reshape(tok, images, features).swapaxes(0, 1)
    return (d_tokens, d_slot_weight, d_gain, d_first[None], d_second[None])


def solution(mesh):
    fine = Mesh(
        mesh.devices.reshape(2, mesh.shape["dp"] // 2, 2, mesh.shape["expert"] // 4, 2),
        ("yh", "z", "yl", "x", "c"),
    )
    everywhere = P(("yh", "z", "yl", "x", "c"), None, None)
    first = P(("yl", "x", "c"), None, ("yh", "z"))
    second = P(("yl", "x", "c"), ("yh", "z"), None)
    return jax.shard_map(
        on_device,
        mesh=fine,
        in_specs=(everywhere, P(), P(), first, second, everywhere),
        out_specs=(everywhere, P(), P(), first, second),
        check_vma=False,
    )
```

```python
import functools

import jax
import jax.numpy as jnp
from jax import lax
from jax.experimental import pallas as pl
from jax.experimental.pallas import tpu as pltpu
from jax.sharding import Mesh
from jax.sharding import PartitionSpec as P

eps = 1e-06
f32 = jnp.float32
bf16 = jnp.bfloat16
VMEM = 60 * 1024 * 1024
RING = 3 * 10**9
RING2 = 3 * 10**9
LOW = 1024 * 1024


def dot(a, b, ca, cb):
    return lax.dot_general(a, b, (((ca,), (cb,)), ((), ())), preferred_element_type=f32)


def own(shape, images):
    row = lax.broadcasted_iota(jnp.int32, shape, 0)
    col = lax.broadcasted_iota(jnp.int32, shape, 1)
    return lax.rem(row, images) == lax.rem(col, images)


def replicated(slot_ref, images):
    slots, features = slot_ref.shape
    rows = jnp.broadcast_to(slot_ref[...].astype(f32)[:, None, :], (slots, images, features))
    return rows.reshape(slots * images, features).astype(bf16)


def cuts(rows, shares):
    groups = rows // 16
    at = 0
    out = []
    for k, share in enumerate(shares):
        size = groups - at if k == len(shares) - 1 else groups * share // sum(shares)
        if size:
            out.append(pl.ds(at * 16, size * 16 if k < len(shares) - 1 else rows - at * 16))
        at += size
    return out


def copies_of(src, dst, sem, slices):
    return [pltpu.make_async_copy(src.at[r], dst.at[r], sem.at[k]) for k, r in enumerate(slices)]


def row_softmax(logits, images):
    mine = own(logits.shape, images)
    ec = jnp.where(mine, jnp.exp(logits - jnp.max(logits, axis=1, keepdims=True)), 0.0)
    return ec / jnp.sum(ec, axis=1, keepdims=True)


def front_kernel(
    shares, gain_ref, slot_ref, x_ref, c_ref, out_ref, normed_ref, acc_ref, col_ref,
    x_s, c_s, out_s, normed_s, lg_s, acc_s, x_sem, c_sem, normed_sem, last_sem,
):
    slots, features = slot_ref.shape
    copies, _, images, _ = out_s.shape
    images = images // 2
    slices = cuts(x_s.shape[0], shares)
    x_in = copies_of(x_ref, x_s, x_sem, slices)
    c_in = copies_of(c_ref, c_s, c_sem, slices)
    normed_out = copies_of(normed_s, normed_ref, normed_sem, slices)
    for one, two in zip(x_in, c_in):
        one.start()
        two.start()
    wrep = replicated(slot_ref, images)
    gain = gain_ref[...]
    cot_slots = 0.0
    for k, r in enumerate(slices):
        x_in[k].wait()
        x = x_s[r].astype(f32)
        xc = x - jnp.mean(x, axis=-1, keepdims=True)
        inv = lax.rsqrt(jnp.mean(xc * xc, axis=-1, keepdims=True) + eps)
        normed = (xc * inv * gain).astype(bf16)
        normed_s[r] = normed
        normed_out[k].start()
        logits = dot(normed, wrep, 1, 1)
        lg_s[r] = logits
        pc = row_softmax(logits, images)
        c_in[k].wait()
        cot_slots = cot_slots + dot(pc.astype(bf16), c_s[r], 0, 0)
    lg = lg_s[...]
    lg = jnp.where(own(lg.shape, images), lg, -jnp.inf)
    most = jnp.max(lg, axis=0, keepdims=True)
    ed = jnp.exp(lg - most)
    total = jnp.sum(ed, axis=0, keepdims=True)
    pd = ed / total
    row = lax.broadcasted_iota(jnp.int32, col_ref.shape, 0)
    col_ref[...] = jnp.where(row == 0, most, total)
    got = dot(pd.astype(bf16), normed_s[...], 0, 0)
    both = [got.reshape(slots, images, features), cot_slots.reshape(slots, images, features)]
    both = jnp.concatenate(both, axis=1).astype(bf16)
    for copy in range(copies):
        out_s[copy] = both
    acc_s[...] = got
    last = [
        pltpu.make_async_copy(src, dst, last_sem.at[j])
        for j, (src, dst) in enumerate(((out_s, out_ref), (acc_s, acc_ref)))
    ]
    for copy in last:
        copy.start()
    for copy in normed_out + last:
        copy.wait()


vmem = pl.BlockSpec(memory_space=pltpu.VMEM)
anywhere = pl.BlockSpec(memory_space=pl.ANY)


def front(tokens, norm_gain, slot_t, cotangent, images, copies, shares=(1, 1)):
    rows, features = tokens.shape
    slots = slot_t.shape[0]
    wide = slots * images
    n = len(shares)
    sent = ((copies, slots, 2 * images, features), bf16)
    acc = ((wide, features), f32)
    return pl.pallas_call(
        functools.partial(front_kernel, shares),
        in_specs=[vmem, vmem, anywhere, anywhere],
        out_specs=[anywhere] * 3 + [vmem],
        out_shape=[
            jax.ShapeDtypeStruct(*sent),
            jax.ShapeDtypeStruct((rows, features), bf16),
            jax.ShapeDtypeStruct(*acc),
            jax.ShapeDtypeStruct((8, wide), f32),
        ],
        scratch_shapes=[pltpu.VMEM(tokens.shape, bf16)] * 2
        + [
            pltpu.VMEM(*sent),
            pltpu.VMEM(tokens.shape, bf16),
            pltpu.VMEM((rows, wide), f32),
            pltpu.VMEM(*acc),
            pltpu.SemaphoreType.DMA((n,)),
            pltpu.SemaphoreType.DMA((n,)),
            pltpu.SemaphoreType.DMA((n,)),
            pltpu.SemaphoreType.DMA((2,)),
        ],
        compiler_params=pltpu.CompilerParams(vmem_limit_bytes=VMEM),
        cost_estimate=pl.CostEstimate(flops=8 * 10**9, bytes_accessed=14 * 2**20, transcendentals=10**6),
        name="front",
    )(norm_gain, slot_t, tokens, cotangent)


gelu_c = 0.7978845608028654
gelu_k = 0.044715


def expert_kernel(n, act_ref, *refs):
    firsts, seconds = refs[:n], refs[n : 2 * n]
    ret_ref, dw_refs = refs[2 * n], refs[2 * n + 1 : 3 * n + 1]
    (
        act_s, w1_s, w2_s, dw_s, ret_s, y_acc, g_acc, act_sem, w1_sem, w2_sem, dw_sem, ret_sem,
    ) = refs[3 * n + 1 :]
    peers, rows, features = act_s.shape
    half = rows // 2
    part = seconds[0].shape[0]
    groups = w1_s.shape[0]
    size = n // groups
    act_copy = pltpu.make_async_copy(act_ref, act_s, act_sem)
    act_copy.start()
    copies = []
    for r in range(n):
        g, q = r // size, r % size
        one = pltpu.make_async_copy(firsts[r], w1_s.at[g, :, pl.ds(q * part, part)], w1_sem.at[r])
        two = pltpu.make_async_copy(seconds[r], w2_s.at[g, pl.ds(q * part, part)], w2_sem.at[r])
        one.start()
        two.start()
        copies.append((one, two))
    act_copy.wait()
    act = act_s[...].astype(f32)
    slots = act[:, :half].reshape(peers * half, features).astype(bf16)
    cots = act[:, half:].reshape(peers * half, features).astype(bf16)
    sends = []
    for g in range(groups):
        for q in range(size):
            copies[g * size + q][0].wait()
            copies[g * size + q][1].wait()
        w1 = w1_s[g]
        w2 = w2_s[g]
        pre = dot(slots, w1, 1, 0)
        sq = pre * pre
        th = jnp.tanh(gelu_c * (pre + gelu_k * (sq * pre)))
        cdf = 0.5 * (1.0 + th)
        hidden = (pre * cdf).astype(bf16)
        slope = cdf + 0.5 * pre * (1.0 - th * th) * (gelu_c * (1.0 + 3.0 * gelu_k * sq))
        d_act = (dot(cots, w2, 1, 1) * slope).astype(bf16)
        y = dot(hidden, w2, 1, 0)
        grad = dot(d_act, w1, 1, 1)
        if g:
            y = y + y_acc[...]
            grad = grad + g_acc[...]
        if g < groups - 1:
            y_acc[...] = y
            g_acc[...] = grad
        else:
            ret_s[...] = jnp.concatenate(
                [y.reshape(peers, half, features), grad.reshape(peers, half, features)], axis=1
            ).astype(bf16)
            ret_copy = pltpu.make_async_copy(ret_s, ret_ref, ret_sem)
            ret_copy.start()
        d_w1 = dot(slots, d_act, 0, 0).astype(bf16)
        d_w2 = dot(hidden, cots, 0, 0).astype(bf16)
        for q in range(size):
            r = g * size + q
            mine = slice(q * part, (q + 1) * part)
            dw_s[r, :features] = d_w1[:, mine]
            for j in range(features // part):
                dw_s[r, pl.ds(features + j * part, part)] = d_w2[mine, j * part : (j + 1) * part]
            send = pltpu.make_async_copy(dw_s.at[r], dw_refs[r], dw_sem.at[r])
            send.start()
            sends.append(send)
    ret_copy.wait()
    for send in sends:
        send.wait()


def expert(act, firsts, seconds):
    peers, rows, features = act.shape
    part = firsts[0].shape[1]
    n = len(firsts)
    all_rows = peers * rows // 2
    size = 4 if n % 4 == 0 else 1
    wide = pltpu.VMEM((n // size, features, size * part), bf16)
    tall = pltpu.VMEM((n // size, size * part, features), bf16)
    got = pl.pallas_call(
        functools.partial(expert_kernel, n),
        in_specs=[anywhere] * (1 + 2 * n),
        out_specs=[anywhere] * (1 + n),
        out_shape=[jax.ShapeDtypeStruct(act.shape, bf16)]
        + [jax.ShapeDtypeStruct((2 * features, part), bf16)] * n,
        scratch_shapes=[
            pltpu.VMEM((peers, rows, features), bf16),
            wide,
            tall,
            pltpu.VMEM((n, 2 * features, part), bf16),
            pltpu.VMEM((peers, rows, features), bf16),
            pltpu.VMEM((all_rows, features), f32),
            pltpu.VMEM((all_rows, features), f32),
            pltpu.SemaphoreType.DMA,
            pltpu.SemaphoreType.DMA((n,)),
            pltpu.SemaphoreType.DMA((n,)),
            pltpu.SemaphoreType.DMA((n,)),
            pltpu.SemaphoreType.DMA,
        ],
        compiler_params=pltpu.CompilerParams(vmem_limit_bytes=VMEM),
        cost_estimate=pl.CostEstimate(flops=4 * 10**9, bytes_accessed=10 * 2**20, transcendentals=10**6),
        name="expert",
    )(act, *firsts, *seconds)
    return got[0], got[1:]


def add_up_kernel(*refs):
    total = 0.0
    for ref in refs[:-1]:
        for k in range(ref.shape[0]):
            total = total + ref[k]
    for k in range(refs[-1].shape[0]):
        refs[-1][k] = total


def add_up(arrays, copies):
    return pl.pallas_call(
        add_up_kernel,
        in_specs=[vmem] * len(arrays),
        out_specs=vmem,
        out_shape=jax.ShapeDtypeStruct((copies, *arrays[0].shape[1:]), f32),
        compiler_params=pltpu.CompilerParams(vmem_limit_bytes=8 * 1024 * 1024),
        cost_estimate=pl.CostEstimate(flops=10**8, bytes_accessed=2**20, transcendentals=0),
        name="add_up",
    )(*arrays)


def finish_kernel(core_ref, mine_ref, other_ref, weight_ref, gain_ref):
    slots, features = weight_ref.shape
    part = mine_ref.shape[1]
    blocks = features // part // 2
    first = core_ref[0] == 0
    mine, other = mine_ref[...], other_ref[...]
    for k, rows in enumerate((jnp.where(first, mine, other), jnp.where(first, other, mine))):
        for j in range(blocks):
            here = slice((k * blocks + j) * part, (k * blocks + j + 1) * part)
            weight_ref[:, here] = rows[j * slots : (j + 1) * slots]
            gain_ref[:, here] = rows[blocks * slots + j : blocks * slots + j + 1]


def finish(core, mine, other, slots, features):
    return pl.pallas_call(
        finish_kernel,
        in_specs=[pl.BlockSpec(memory_space=pltpu.SMEM), vmem, vmem],
        out_specs=[vmem] * 2,
        out_shape=[jax.ShapeDtypeStruct((slots, features), f32), jax.ShapeDtypeStruct((1, features), f32)],
        compiler_params=pltpu.CompilerParams(vmem_limit_bytes=8 * 1024 * 1024),
        cost_estimate=pl.CostEstimate(flops=10**6, bytes_accessed=2**18, transcendentals=0),
        name="finish",
    )(core, mine, other)


def route_kernel(
    shares, core_ref, gain_ref, slot_ref, col_ref, c_ref, normed_ref, ret_ref, acc_ref,
    mine_ref, other_ref, gain_out, coef_ref, grad_ref,
    c_s, normed_s, ret_s, acc_s, coef_s, grad_s, out_s, pd_s, dd_s, fc_s,
    c_sem, normed_sem, whole_sem, coef_sem,
):
    copies, slots, images, features = ret_s.shape
    images = images // 2
    wide = slots * images
    slices = cuts(c_s.shape[0], shares)
    c_in = copies_of(c_ref, c_s, c_sem, slices)
    normed_in = copies_of(normed_ref, normed_s, normed_sem, slices)
    coef_out = copies_of(coef_s, coef_ref, coef_sem, slices)
    ret_in = pltpu.make_async_copy(ret_ref, ret_s, whole_sem.at[0])
    acc_in = pltpu.make_async_copy(acc_ref, acc_s, whole_sem.at[1])
    grad_out = pltpu.make_async_copy(grad_s, grad_ref, whole_sem.at[2])
    ret_in.start()
    for one, two in zip(normed_in, c_in):
        one.start()
        two.start()
    acc_in.start()
    wrep = replicated(slot_ref, images)
    grad_s[wide:] = wrep
    most, total = col_ref[0:1], col_ref[1:2]
    ret_in.wait()
    got = ret_s[0].astype(f32)
    for copy in range(1, copies):
        got = got + ret_s[copy].astype(f32)
    out_s[...] = got[:, :images].reshape(wide, features).astype(bf16)
    grad_s[:wide] = got[:, images:].reshape(wide, features).astype(bf16)
    grad_out.start()
    col_sum = jnp.zeros((1, wide), f32)
    for k, r in enumerate(slices):
        normed_in[k].wait()
        logits = dot(normed_s[r], wrep, 1, 1)
        pc = row_softmax(logits, images)
        pd = jnp.where(own(logits.shape, images), jnp.exp(logits - most) / total, 0.0)
        dd = dot(normed_s[r], grad_s[:wide], 1, 1)
        c_in[k].wait()
        d_combine = dot(c_s[r], out_s[...], 1, 1)
        fc_s[r] = pc * (d_combine - jnp.sum(pc * d_combine, axis=1, keepdims=True))
        pd_s[r] = pd
        dd_s[r] = dd
        col_sum = col_sum + jnp.sum(pd * dd, axis=0, keepdims=True)
    for k, r in enumerate(slices):
        pd = pd_s[r]
        coef_s[r, :wide] = pd.astype(bf16)
        coef_s[r, wide:] = (fc_s[r] + pd * (dd_s[r] - col_sum)).astype(bf16)
        coef_out[k].start()
    acc = dot(coef_s[:, wide:], normed_s[...], 0, 0)
    acc_in.wait()
    d_weight = jnp.sum(acc.reshape(slots, images, features), axis=1)
    d_gain = jnp.sum(acc_s[...] * grad_s[:wide].astype(f32), axis=0, keepdims=True)
    d_gain = d_gain + jnp.sum(acc * grad_s[wide:].astype(f32), axis=0, keepdims=True)
    d_gain = d_gain / gain_ref[...]
    part = mine_ref.shape[1]
    blocks = features // part // 2
    first = core_ref[0] == 0
    gain_out[...] = gain_ref[...]

    def chosen(j, rows):
        low = rows[:, j * part : (j + 1) * part]
        high = rows[:, (blocks + j) * part : (blocks + j + 1) * part]
        return jnp.where(first, low, high), jnp.where(first, high, low)

    for j in range(blocks):
        here = slice(j * slots, (j + 1) * slots)
        mine_ref[here], other_ref[here] = chosen(j, d_weight)
    last = [chosen(j, d_gain) for j in range(blocks)]
    rest = jnp.zeros((8 - blocks, part), f32)
    mine_ref[blocks * slots :] = jnp.concatenate([one for one, _ in last] + [rest], axis=0)
    other_ref[blocks * slots :] = jnp.concatenate([two for _, two in last] + [rest], axis=0)
    for copy in coef_out:
        copy.wait()
    grad_out.wait()


def route(core, cotangent, normed, norm_gain, slot_t, col, ret, acc, shares=(1, 1)):
    rows, features = cotangent.shape
    _, slots, images, _ = ret.shape
    wide = slots * images // 2
    n = len(shares)
    ins = (cotangent, normed, ret, acc)
    outs = [((rows, 2 * wide), bf16), ((2 * wide, features), bf16)]
    sums = jax.ShapeDtypeStruct((features // 256 * slots + 8, 128), f32)
    return pl.pallas_call(
        functools.partial(route_kernel, shares),
        in_specs=[pl.BlockSpec(memory_space=pltpu.SMEM)] + [vmem] * 3 + [anywhere] * len(ins),
        out_specs=[vmem] * 3 + [anywhere] * len(outs),
        out_shape=[sums] * 2 + [jax.ShapeDtypeStruct(norm_gain.shape, f32)] + [jax.ShapeDtypeStruct(*out) for out in outs],
        scratch_shapes=[pltpu.VMEM(x.shape, x.dtype) for x in ins]
        + [pltpu.VMEM(*out) for out in outs]
        + [
            pltpu.VMEM((wide, features), bf16),
            pltpu.VMEM((rows, wide), f32),
            pltpu.VMEM((rows, wide), f32),
            pltpu.VMEM((rows, wide), f32),
            pltpu.SemaphoreType.DMA((n,)),
            pltpu.SemaphoreType.DMA((n,)),
            pltpu.SemaphoreType.DMA((3,)),
            pltpu.SemaphoreType.DMA((n,)),
        ],
        compiler_params=pltpu.CompilerParams(vmem_limit_bytes=VMEM),
        cost_estimate=pl.CostEstimate(flops=5 * 10**9, bytes_accessed=14 * 2**20, transcendentals=0),
        name="route",
    )(core, norm_gain, slot_t, col, *ins)


def back_kernel(gain_ref, grad_ref, x_ref, coef_ref, dt_ref):
    x = x_ref[...].astype(f32)
    xc = x - jnp.mean(x, axis=-1, keepdims=True)
    inv = lax.rsqrt(jnp.mean(xc * xc, axis=-1, keepdims=True) + eps)
    x_hat = xc * inv
    scaled = dot(coef_ref[...], grad_ref[...], 1, 0) * gain_ref[...]
    mean_scaled = jnp.mean(scaled, axis=-1, keepdims=True)
    mean_dot = jnp.mean(scaled * x_hat, axis=-1, keepdims=True)
    dt_ref[...] = (inv * (scaled - mean_scaled - x_hat * mean_dot)).astype(bf16)


def back(tokens, coef, norm_gain, grad):
    rows, features = tokens.shape
    wide = coef.shape[1]
    steps = 2 if rows % 32 == 0 else 1
    block = pl.BlockSpec((rows // steps, features), lambda i: (i, 0))
    return pl.pallas_call(
        back_kernel,
        grid=(steps,),
        in_specs=[
            pl.BlockSpec((1, features), lambda i: (0, 0)),
            pl.BlockSpec((wide, features), lambda i: (0, 0)),
            block,
            pl.BlockSpec((rows // steps, wide), lambda i: (i, 0)),
        ],
        out_specs=block,
        out_shape=jax.ShapeDtypeStruct(tokens.shape, bf16),
        compiler_params=pltpu.CompilerParams(vmem_limit_bytes=VMEM),
        cost_estimate=pl.CostEstimate(flops=5 * 10**9, bytes_accessed=8 * 2**20, transcendentals=0),
        name="back",
    )(norm_gain, grad, tokens, coef)


def gate_kernel(*refs):
    pass


def after(kept, others, weight=0, limit=None):
    return pl.pallas_call(
        gate_kernel,
        in_specs=[anywhere] * (len(kept) + len(others)),
        out_specs=[anywhere] * len(kept),
        out_shape=[jax.ShapeDtypeStruct(x.shape, x.dtype) for x in kept],
        input_output_aliases={i: i for i in range(len(kept))},
        compiler_params=pltpu.CompilerParams(vmem_limit_bytes=limit),
        cost_estimate=pl.CostEstimate(flops=weight, bytes_accessed=0, transcendentals=0),
        name="after",
    )(*kept, *others)


def on_device(tokens, norm_gain, slot_weight, w_in, w_out, cotangent):
    images, _, features = tokens.shape
    slots = slot_weight.shape[1]
    part = w_in.shape[2]
    halves = lax.axis_size("yh")
    peers = ("yh", "yl", "x", "c")

    n = lax.axis_size("z")
    up = [(i, (i + 1) % n) for i in range(n)]
    down = [(i, (i - 1) % n) for i in range(n)]
    firsts = {0: w_in[0]}
    seconds = {0: w_out[0]}

    def step(k):
        firsts[n - k] = lax.ppermute(firsts[(n - k + 1) % n], "z", up)
        seconds[k] = lax.ppermute(seconds[k - 1], "z", down)
        if k < n - k:
            firsts[k] = lax.ppermute(firsts[k - 1], "z", down)
            seconds[n - k] = lax.ppermute(seconds[(n - k + 1) % n], "z", up)

    step(1)
    gain = norm_gain[None]
    slot_t = slot_weight.T
    tok = tokens.shape[1]
    by_place = tokens.swapaxes(0, 1).reshape(tok * images, features)
    cots = cotangent.swapaxes(0, 1).reshape(tok * images, features)
    sent, normed, acc, col = front(by_place, gain, slot_t, cots, images, halves)
    sent, firsts[1], firsts[n - 1], seconds[1], seconds[n - 1] = after(
        [sent, firsts[1], firsts[n - 1], seconds[1], seconds[n - 1]], []
    )
    act = lax.all_to_all(
        sent.reshape(halves * slots, 2 * images, features), peers, 0, 0, tiled=True
    )
    for k in range(2, n // 2 + 1):
        step(k)
    far = n // 2
    firsts[far], seconds[far] = after([firsts[far], seconds[far]], [], RING)
    if n > 3:
        firsts[far - 1], seconds[far + 1] = after([firsts[far - 1], seconds[far + 1]], [], RING2)
    ret, d_w = expert(act, [firsts[r] for r in range(n)], [seconds[r] for r in range(n)])
    ret = lax.all_to_all(ret, peers, 0, 0, tiled=True)

    state = [d_w[far], d_w[(far + 1) % n]]

    def pass_on(k):
        state[0] = lax.ppermute(state[0], "z", up)
        if k < far:
            state[1] = lax.ppermute(state[1], "z", down)

    def add_own(k):
        state[0] = state[0] + d_w[far - k]
        if k < far - 1:
            state[1] = state[1] + d_w[far + 1 + k]

    pass_on(1)
    if far > 2:
        add_own(1)
        pass_on(2)
    done = 2 if far > 2 else 1

    core = lax.axis_index("c")
    swap = [(0, 1), (1, 0)]
    ret = ret.reshape(halves, slots, 2 * images, features)
    mine, other, late_gain, coef, grad = route(core.reshape(1), cots, normed, gain, slot_t, col, ret, acc)
    plane = ("yh", "yl", "x")
    n_plane = halves * lax.axis_size("yl") * lax.axis_size("x")
    copies = add_up([mine[None], lax.ppermute(other, "c", swap)[None]], n_plane)
    state = list(after(state, [copies], limit=LOW))
    copies = lax.all_to_all(copies, plane, 0, 0, tiled=True)
    for k in range(done, far):
        add_own(k)
        pass_on(k + 1)
    copies = add_up([copies], n)
    (late_gain,) = after([late_gain], [copies], limit=LOW)
    d_tokens = back(by_place, coef, late_gain, grad)
    (share,) = add_up([lax.all_to_all(copies, "z", 0, 0, tiled=True)], 1)
    pieces = features // part
    total = (d_w[0].astype(f32) + state[0].astype(f32)) + state[1].astype(f32)
    d_first = total[:features]
    d_second = total[features:].reshape(pieces, part, part).swapaxes(0, 1).reshape(part, features)
    other = lax.ppermute(share, "c", swap)
    d_slot_weight, d_gain = finish(core.reshape(1), share, other, slots, features)
    d_slot_weight = d_slot_weight.T
    d_gain = d_gain.reshape(features)
    d_tokens = d_tokens.reshape(tok, images, features).swapaxes(0, 1)
    return (d_tokens, d_slot_weight, d_gain, d_first[None], d_second[None])


def solution(mesh):
    fine = Mesh(
        mesh.devices.reshape(2, mesh.shape["dp"] // 2, 2, mesh.shape["expert"] // 4, 2),
        ("yh", "z", "yl", "x", "c"),
    )
    everywhere = P(("yh", "z", "yl", "x", "c"), None, None)
    first = P(("yl", "x", "c"), None, ("yh", "z"))
    second = P(("yl", "x", "c"), ("yh", "z"), None)
    return jax.shard_map(
        on_device,
        mesh=fine,
        in_specs=(everywhere, P(), P(), first, second, everywhere),
        out_specs=(everywhere, P(), P(), first, second),
        check_vma=False,
    )
```
